32 devices in a mesh: grp: 2 (over x), shot: 8 (over z, y), depth: 2 (over core).
Axes of the slice: x: 2, y: 2, z: 4, core: 2. Of those that a mesh axis runs over, the one named last changes fastest.
Arguments:
- wave_prev: float32 [16, 32, 128, 128], P(('grp', 'shot'), 'depth'), parts along dimension 0, may hold values from -6 to 6
- wave_now: float32 [16, 32, 128, 128], P(('grp', 'shot'), 'depth'), parts along dimension 0, may hold values from -6 to 6
- adjoint: float32 [16, 4, 32, 128, 128], P(('grp', 'shot'), None, 'depth'), parts along dimension 0, may hold values from -6 to 6
- coarse_velocity: float32 [32, 4096], P(('grp', 'depth'), 'shot'), parts along dimension 0, may hold values from 1.5 to 4.5
- filters: float32 [16, 27], replicated, may hold values from -1.25 to 1.25
- wavelet: float32 [16, 4], P(('grp', 'shot')), parts along dimension 0, may hold values from -30 to 30
- source_cell: int32 [16], P(('grp', 'shot')), parts along dimension 0, may hold values from 0 to 524287
- receiver_cells: int32 [16, 128], P(('grp', 'shot')), parts along dimension 0, may hold values from 0 to 524287
Outputs:
- gradient: float32 [32, 4096], P(('grp', 'depth'), 'shot'), parts along dimension 0
- wave_prev_out: float32 [16, 32, 128, 128], P(('grp', 'shot'), 'depth'), parts along dimension 0
- wave_now_out: float32 [16, 32, 128, 128], P(('grp', 'shot'), 'depth'), parts along dimension 0
- traces: float32 [16, 4, 128], P(('grp', 'shot')), parts along dimension 0
The draws below stay inside these ranges and needn't reach their ends.
There are 2 independent parts, one for each index of `grp`. The reference program is written for one: setup_inputs(seed, part) draws one part's arguments, and reference() takes and returns one part's arrays. A program takes and returns all parts, laid end to end along the dimension named above; an argument that names none is the same for every part. Nothing has to cross between parts.
All inputs are finite; a program needn't handle non-finite values.
Results may differ from the reference program's by a relative error of at most 0.0003.
Values sent between devices are 32-bit elements; how exact they have to be, the bound alone decides.
A program may use at most 192 MiB of HBM per device.

```python
import jax
import jax.numpy as jnp
from jax import lax

NX = 128
NY = 128
STEPS = 4
CHANNELS = 16
NREC = 128
SHOTS = 8
NZ = 32
ZC = 16
XC = 64
YC = 64


def with_ends(entries, own_key, smallest, top_value):
    longest = entries.shape.index(max(entries.shape))
    spots = []
    for shift in (0, 1):
        where = [jax.random.randint(jax.random.fold_in(own_key, axis), (), 0, length) for axis, length in enumerate(entries.shape)]
        where[longest] = (where[longest] + shift) % entries.shape[longest]
        spots.append(tuple(where))
    return entries.at[spots[0]].set(smallest).at[spots[1]].set(top_value)


def block_levels(key, extent, shards, least, high):
    def one(dim, blocks):
        draws = jax.random.uniform(jax.random.fold_in(jax.random.fold_in(key, 6), dim), (blocks,), jnp.float32, least / len(shards), high / len(shards))
        return jnp.repeat(jnp.exp(draws), extent[dim] // blocks).reshape((-1,) + (1,) * (len(extent) - dim - 1))

    level = one(*shards[0])
    for cut in shards[1:]:
        level = level * one(*cut)
    return level


def gaussian(own_key, extent, width, limit, pieces=(), kind=jnp.bfloat16):
    result = jax.random.normal(own_key, extent, jnp.float32) * width
    if len(pieces) > 0:
        result = block_levels(own_key, extent, pieces, -0.22, 0.18) * result
    return jnp.clip(result, min=-limit, max=limit).astype(kind)


def setup_inputs(seed: int = 0, part: int = 0) -> dict:
    key_of = jax.random.split(jax.random.key(seed), 9)
    part_keys = jax.random.split(jax.random.fold_in(key_of[8], part), 9)
    wave_prev = gaussian(part_keys[0], (SHOTS, NZ, NX, NY), 1.0, 6.0, ((0, 8), (1, 2)), jnp.float32)
    wave_now = gaussian(part_keys[1], (SHOTS, NZ, NX, NY), 1.0, 6.0, ((0, 8), (1, 2)), jnp.float32)
    adjoint = gaussian(part_keys[2], (SHOTS, STEPS, NZ, NX, NY), 1.0, 6.0, ((0, 8), (2, 2)), jnp.float32)
    coarse_velocity = jnp.clip(1.5 + 3.0 * jax.random.uniform(part_keys[3], (ZC, XC * YC), jnp.float32) ** block_levels(part_keys[3], (ZC, XC * YC), ((0, 2), (1, 8)), -0.2, 0.2), 1.5, 4.5)
    filters = gaussian(key_of[4], (CHANNELS, 27), 27 ** -0.5, 1.25, (), jnp.float32)
    wavelet = gaussian(part_keys[5], (SHOTS, STEPS), 5.0, 30.0, ((0, 8),), jnp.float32)
    source_cell = with_ends(jax.random.randint(part_keys[6], (SHOTS,), 0, NZ * NX * NY), jax.random.fold_in(part_keys[6], 1), 0, (NZ * NX * NY) - 1).astype(jnp.int32)
    receiver_cells = with_ends(jax.random.randint(part_keys[7], (SHOTS, NREC), 0, NZ * NX * NY), jax.random.fold_in(part_keys[7], 1), 0, (NZ * NX * NY) - 1).astype(jnp.int32)
    return {"wave_prev": wave_prev, "wave_now": wave_now, "adjoint": adjoint, "coarse_velocity": coarse_velocity, "filters": filters, "wavelet": wavelet, "source_cell": source_cell, "receiver_cells": receiver_cells}


coeffs = (-205.0 / 72.0, 8.0 / 5.0, -1.0 / 5.0, 8.0 / 315.0, -1.0 / 560.0)
courant = 0.1
offsets = [(a, b, c) for a in (-1, 0, 1) for b in (-1, 0, 1) for c in (-1, 0, 1)]


def stencil(padded, row_count):
    width_x, width_y = padded.shape[1], padded.shape[2]
    lateral = jnp.pad(padded, ((0, 0), (4, 4), (4, 4)))

    def window(shift_z, shift_x, shift_y):
        return lateral[4 + shift_z:4 + shift_z + row_count, 4 + shift_x:4 + shift_x + width_x, 4 + shift_y:4 + shift_y + width_y]

    summed = 3.0 * coeffs[0] * window(0, 0, 0)
    for reach in range(1, 5):
        pairs = window(reach, 0, 0) + window(-reach, 0, 0) + window(0, reach, 0) + window(0, -reach, 0) + window(0, 0, reach) + window(0, 0, -reach)
        summed = summed + coeffs[reach] * pairs
    return summed


def upsample(coarse, half_x, half_y):
    brick_view = coarse.reshape(coarse.shape[0], half_x, half_y)
    return jnp.repeat(jnp.repeat(jnp.repeat(brick_view, 2, 0), 2, 1), 2, 2)


def coarsen(fine_field):
    depth_rows, width_x, width_y = fine_field.shape
    grouped = fine_field.reshape(depth_rows // 2, 2, width_x // 2, 2, width_y // 2, 2).sum(axis=(1, 3, 5))
    return grouped.reshape(depth_rows // 2, (width_x // 2) * (width_y // 2))


def shifted(widened, a, b, c, row_count, half_y):
    column_total = widened.shape[-1] - 2 * (half_y + 1)
    offset = half_y + 1 + b * half_y + c
    window = widened[1 + a:1 + a + row_count, offset:offset + column_total]
    column = jnp.arange(column_total, dtype=jnp.int32) % half_y
    inside = (column + c >= 0) & (column + c < half_y)
    return jnp.where(inside[None, :], window, 0.0)


def prior_scores(padded, row_count, half_y, filters):
    widened = jnp.pad(padded, ((0, 0), (half_y + 1, half_y + 1)))
    stacked = jnp.stack([shifted(widened, a, b, c, row_count, half_y) for (a, b, c) in offsets])
    scores = jnp.einsum("kt,tzn->kzn", filters, stacked, precision=lax.Precision.HIGHEST)
    return scores / (1.0 + scores * scores)


def prior_back(response_pad, row_count, half_y, filters):
    spread = jnp.einsum("kt,kzn->tzn", filters, response_pad, precision=lax.Precision.HIGHEST)
    widened = jnp.pad(spread, ((0, 0), (0, 0), (half_y + 1, half_y + 1)))
    summed = jnp.zeros((row_count, spread.shape[-1]), spread.dtype)
    for position, (a, b, c) in enumerate(offsets):
        summed = summed + shifted(widened[position], -a, -b, -c, row_count, half_y)
    return summed


def reference(wave_prev, wave_now, adjoint, coarse_velocity, filters, wavelet, source_cell, receiver_cells):
    velocity = upsample(coarse_velocity, XC, YC)
    speed_term = (courant * velocity) ** 2
    cell_index = jnp.arange(NZ * NX * NY, dtype=jnp.int32).reshape(NZ, NX, NY)

    def one_shot(inputs):
        earlier, current, adjoints, pulses, source, receivers = inputs
        source_hit = cell_index == source
        imaging = jnp.zeros_like(current)
        trace_rows = []
        for moment in range(STEPS):
            padded = jnp.pad(current, ((4, 4), (0, 0), (0, 0)))
            laplace = stencil(padded, NZ)
            following = 2.0 * current - earlier + speed_term * laplace + jnp.where(source_hit, speed_term * pulses[moment], 0.0)
            imaging = imaging + adjoints[moment] * (following - 2.0 * current + earlier)
            trace_rows.append(following.reshape(-1)[receivers])
            earlier, current = current, following
        fine_grad = -2.0 * imaging / velocity ** 3
        return earlier, current, jnp.stack(trace_rows), coarsen(fine_grad)

    last_prev, last_now, traces, shot_terms = lax.map(one_shot, (wave_prev, wave_now, adjoint, wavelet, source_cell, receiver_cells))
    image_grad = jnp.sum(shot_terms, axis=0)
    response = prior_scores(jnp.pad(coarse_velocity, ((1, 1), (0, 0))), ZC, YC, filters)
    response_pad = jnp.pad(response, ((0, 0), (1, 1), (0, 0)))
    prior_grad = prior_back(response_pad, ZC, YC, filters)
    return image_grad + prior_grad, last_prev, last_now, traces
```

```python
import functools

import jax
import jax.numpy as jnp
from jax import lax
from jax.experimental import pallas as pl
from jax.experimental.pallas import tpu as pltpu
from jax.sharding import PartitionSpec as P

coeffs = (-205.0 / 72.0, 8.0 / 5.0, -1.0 / 5.0, 8.0 / 315.0, -1.0 / 560.0)
courant = 0.1
HALO = 4
f32, bf16, i32 = jnp.float32, jnp.bfloat16, jnp.int32
NT = (((1,), (1,)), ((), ()))
TN = (((0,), (0,)), ((), ()))


def iota(shape, dim):
    return lax.broadcasted_iota(i32, shape, dim)


def split(value, parts):
    out = []
    for _ in range(parts - 1):
        part = value.astype(bf16)
        value = value - part.astype(f32)
        out.append(part)
    return out + [value.astype(bf16)]


def mm(a, b):
    return jnp.dot(a, b, preferred_element_type=f32)


def kernel(
    shots, steps,
    prev_hbm, now_hbm, adj_hbm, cv, filt, wav, src, rec_s, rec_v,
    grad, pout, nout, traces,
    *scratch,
):
    fields = scratch[: steps + 2]
    adjs = scratch[steps + 2 : 2 * steps + 2]
    (
        speed, acc, bx, by, lat, vel, velf, wown, wother, zx, xm, fhi, flo, sb,
        tmp, terms, arrived, picked, tr_own, tr_other,
        in_sem, out_sem, h_send, h_recv, v_send, v_recv, r_send, r_recv, w_sem, t_sem,
    ) = scratch[2 * steps + 2 :]
    rows, wx, wy = adjs[0].shape
    zc_rows, ncol = cv.shape
    half_y = wy // 2
    tiles = ncol // wy
    pairs_x = shots * tiles
    chans = filt.shape[0]
    me_s, me_d = lax.axis_index("shot"), lax.axis_index("depth")
    other = {"depth": 1 - me_d}
    MESH = pl.DeviceIdType.MESH

    def peer(k):
        return lax.rem(me_s + k, shots)

    load_now = pltpu.make_async_copy(now_hbm.at[0], fields[1].at[pl.ds(HALO, rows)], in_sem.at[0])
    load_prev = pltpu.make_async_copy(prev_hbm.at[0], fields[0].at[pl.ds(HALO, rows)], in_sem.at[1])
    load_adj = [
        pltpu.make_async_copy(adj_hbm.at[0, t], adjs[t], in_sem.at[2 + t]) for t in range(steps)
    ]
    load_now.start()
    load_prev.start()
    for c in load_adj:
        c.start()

    barrier = pltpu.get_barrier_semaphore()
    for k in range(1, shots):
        pl.semaphore_signal(barrier, inc=1, device_id={"shot": peer(k)}, device_id_type=MESH)
    pl.semaphore_signal(barrier, inc=1, device_id=other, device_id_type=MESH)
    pl.semaphore_wait(barrier, shots)

    def vel_copy(k, slot, to):
        return pltpu.make_async_remote_copy(
            src_ref=cv, dst_ref=vel.at[slot], send_sem=v_send.at[k], recv_sem=v_recv.at[k],
            device_id={"shot": to}, device_id_type=MESH,
        )

    for k in range(1, shots):
        vel_copy(k, me_s, peer(k)).start()
    inner = jnp.where(me_d == 0, rows - HALO, 0)
    far = jnp.where(me_d == 0, 0, rows + HALO)
    first_halo = pltpu.make_async_remote_copy(
        src_ref=now_hbm.at[0, pl.ds(inner, HALO)], dst_ref=fields[1].at[pl.ds(far, HALO)],
        send_sem=h_send.at[0], recv_sem=h_recv.at[0], device_id=other, device_id_type=MESH,
    )
    first_halo.start()

    for t in range(steps):
        fields[t + 1][pl.ds(far, HALO)] = jnp.zeros((HALO, wx, wy), f32)
    gap_x = jnp.abs(iota((wx, wx), 0) - iota((wx, wx), 1))
    gap_y = jnp.abs(iota((wy, wy), 0) - iota((wy, wy), 1))

    def band(gap):
        value = jnp.where(gap == 0, 1.5 * coeffs[0], 0.0).astype(f32)
        for k in range(1, 5):
            value = jnp.where(gap == k, coeffs[k], value)
        return split(value, 2)

    high, low = band(gap_x)
    bx[...] = jnp.concatenate([high, high, low], axis=1)
    high, low = band(gap_y)
    by[...] = jnp.concatenate([high, high, low], axis=0)

    width = chans * half_y
    spread = (iota((chans, width), 1) // half_y == iota((chans, width), 0)).astype(f32)
    taps = lax.dot_general(
        filt[...], spread, TN, precision=lax.Precision.HIGHEST, preferred_element_type=f32
    )
    taps_hi = taps.astype(bf16).astype(f32)
    taps_lo = taps - taps_hi
    shift_y = iota((half_y, width), 0) - iota((half_y, width), 1) % half_y
    for ab in range(9):
        for weights, out in ((taps_hi, fhi), (taps_lo, flo)):
            value = jnp.zeros((half_y, width), f32)
            for e in (-1, 0, 1):
                value = jnp.where(shift_y == e, weights[3 * ab + e + 1 : 3 * ab + e + 2], value)
            value = value.astype(bf16)
            out[pl.ds(ab * wy, half_y), :] = value
            out[pl.ds(ab * wy + half_y, half_y), :] = value

    vel[pl.ds(me_s, 1)] = cv[...][None]
    for k in range(1, shots):
        from_s = lax.rem(me_s + shots - k, shots)
        vel_copy(k, from_s, peer(k)).wait_recv()
    stacked = jnp.concatenate(
        [vel[s, :, q * wy : (q + 1) * wy] for s in range(shots) for q in range(tiles)], axis=0
    )
    up_row, up_col = iota((wy, 2 * wy), 0), iota((wy, 2 * wy), 1)
    up = (up_row == up_col // wy * half_y + up_col % wy // 2).astype(f32).astype(bf16)
    fine = mm(
        jnp.concatenate(split(stacked, 3), axis=1), jnp.concatenate([up, up, up], axis=0)
    )
    velf[0] = fine[:, :wy]
    velf[1] = fine[:, wy:]
    for z in range(zc_rows):
        for i in range(2):
            plane = courant * velf[i, pl.ds(z, pairs_x, stride=zc_rows), :]
            plane = plane * plane
            for j in range(2):
                speed[z, pl.ds(2 * i + j, pairs_x, stride=4), :] = plane

    before = vel[jnp.maximum(me_s - 1, 0), :, ncol - wy :]
    after = vel[jnp.minimum(me_s + 1, shots - 1), :, :wy]
    wown[0] = jnp.where(me_s > 0, before, 0.0)
    for q in range(tiles):
        wown[q + 1] = cv[:, q * wy : (q + 1) * wy]
    wown[tiles + 1] = jnp.where(me_s < shots - 1, after, 0.0)
    w_copy = pltpu.make_async_remote_copy(
        src_ref=wown, dst_ref=wother, send_sem=w_sem.at[0], recv_sem=w_sem.at[1],
        device_id=other, device_id_type=MESH,
    )
    w_copy.start()

    hit = src[0]
    hit_z = hit // (wx * wy) - me_d * rows
    hit_x = hit // wy % wx
    hit_y = hit % wy
    spot = ((iota((wx, wy), 0) == hit_x) & (iota((wx, wy), 1) == hit_y)).astype(f32)
    tmp[...] = spot
    chunk = 32

    def pair(t, zc):
        current, earlier, following = fields[t + 1], fields[t], fields[t + 2]
        z0 = 2 * zc
        halves = [split(current[z0 + HALO + i], 2) for i in range(2)]
        wide = [jnp.concatenate([halves[0][h], halves[1][h]], axis=1) for h in range(2)]
        tall = [jnp.concatenate([halves[0][h], halves[1][h]], axis=0) for h in range(2)]
        along_x = mm(bx[...], jnp.concatenate([wide[0], wide[1], wide[0]], axis=0))
        along_y = mm(jnp.concatenate([tall[0], tall[1], tall[0]], axis=1), by[...])
        for i in range(2):
            lat[i] = along_x[:, i * wy : (i + 1) * wy] + along_y[i * wx : (i + 1) * wx]
        for r in range(0, wx, chunk):
            cut = pl.ds(r, chunk)
            speed_cut = speed[zc, cut, :]
            spot_cut = tmp[cut, :]
            image = None
            planes = [current[z0 + k, cut, :] for k in range(2 * HALO + 2)]
            for i in range(2):
                pulse = jnp.where(hit_z == z0 + i, wav[0, t], 0.0)
                lap = lat[i, cut, :] + spot_cut * pulse
                for k in range(1, 5):
                    lap = lap + coeffs[k] * (planes[i + HALO + k] + planes[i + HALO - k])
                following[z0 + i + HALO, cut, :] = (
                    2.0 * planes[i + HALO] - earlier[z0 + i + HALO, cut, :] + speed_cut * lap
                )
                term = adjs[t][z0 + i, cut, :] * lap
                image = term if image is None else image + term
            if t == 0:
                acc[zc, cut, :] = image
            else:
                acc[zc, cut, :] = acc[zc, cut, :] + image

    edge_pairs = HALO // 2
    inside_pairs = rows // 2 - edge_pairs
    inside_first = me_d * edge_pairs
    edge_first = jnp.where(me_d == 0, inside_pairs, 0)
    halo = first_halo
    sent = [first_halo]
    load_now.wait()
    load_prev.wait()
    stores = []
    for t in range(steps):
        load_adj[t].wait()

        @pl.loop(0, inside_pairs)
        def _(i):
            pair(t, inside_first + i)

        halo.wait_recv()

        @pl.loop(0, edge_pairs)
        def _(i):
            pair(t, edge_first + i)

        if t + 1 < steps:
            halo = pltpu.make_async_remote_copy(
                src_ref=fields[t + 2].at[pl.ds(inner + HALO, HALO)],
                dst_ref=fields[t + 2].at[pl.ds(far, HALO)],
                send_sem=h_send.at[t + 1], recv_sem=h_recv.at[t + 1],
                device_id=other, device_id_type=MESH,
            )
            halo.start()
            sent.append(halo)
        if t + 2 >= steps:
            out = pout if t + 2 == steps else nout
            store = pltpu.make_async_copy(
                fields[t + 2].at[pl.ds(HALO, rows)], out.at[0], out_sem.at[t + 2 - steps]
            )
            store.start()
            stores.append(store)

    fold_row, fold_col = iota((wy, wy), 0), iota((wy, wy), 1)
    fold = (fold_row // 2 == fold_col % half_y).astype(f32).astype(bf16)
    fold = jnp.concatenate([fold, fold], axis=0)
    left = iota((1, wy), 1) < half_y
    for z in range(zc_rows):
        tmp[...] = mm(jnp.concatenate(split(acc[z], 2), axis=1), fold)
        quarter = [tmp[pl.ds(j, pairs_x, stride=4), :] for j in range(4)]
        terms[pl.ds(z, pairs_x, stride=zc_rows), :] = jnp.where(
            left, quarter[0] + quarter[1], quarter[2] + quarter[3]
        )
    block = tiles * zc_rows

    def term_copy(k, slot, to):
        return pltpu.make_async_remote_copy(
            src_ref=terms.at[pl.ds(pl.multiple_of(to * block, 8), block)],
            dst_ref=arrived.at[slot], send_sem=r_send.at[k], recv_sem=r_recv.at[k],
            device_id={"shot": to}, device_id_type=MESH,
        )

    for k in range(1, shots):
        term_copy(k, me_s, peer(k)).start()

    plane_size = wx * wy
    top = rows * plane_size - 1

    @pl.loop(0, rec_s.shape[1])
    def _(r):
        cell = jnp.clip(rec_s[0, r] - me_d * rows * plane_size, 0, top)
        z, x = cell // plane_size, cell // wy % wx
        for t in range(steps):
            picked[t, pl.ds(r, 1), :] = fields[t + 2][z + HALO, pl.ds(x, 1), :]

    cells = rec_v[...] - me_d * rows * plane_size
    inside = (cells >= 0) & (cells <= top)
    count = rec_s.shape[1]
    lane_hit = (iota((wy, count), 0) == jnp.clip(cells, 0, top) % wy) & inside
    tr_own[...] = jnp.zeros_like(tr_own)
    for t in range(steps):
        flipped = jnp.where(lane_hit, picked[t].T, 0.0)
        tr_own[pl.ds(t, 1), :] = jnp.sum(flipped, axis=0, keepdims=True)
    t_copy = pltpu.make_async_remote_copy(
        src_ref=tr_own, dst_ref=tr_other, send_sem=t_sem.at[0], recv_sem=t_sem.at[1],
        device_id=other, device_id_type=MESH,
    )
    t_copy.start()

    w_copy.wait_recv()
    for g in range(tiles + 2):
        own, near = wown[g], wother[g]
        tall = jnp.concatenate(
            [jnp.where(me_d == 0, 0.0, near), own, jnp.where(me_d == 0, near, 0.0)], axis=0
        )
        turned = pltpu.roll(tall, half_y, axis=1)
        for i, both in enumerate((jnp.where(left, tall, turned), jnp.where(left, turned, tall))):
            part = both.astype(bf16).astype(f32)
            zx[2 * g + i] = jnp.where(left, part, both - part)
    out_x = 2 * tiles + 2
    deep = 2 * zc_rows

    @pl.loop(0, out_x)
    def _(j):
        for a in range(3):
            for b in range(3):
                ab = 3 * a + b
                xm[pl.ds(pl.multiple_of(j * deep, 16), deep), ab * wy : (ab + 1) * wy] = zx[
                    j + b, zc_rows - 2 + a : zc_rows - 2 + a + deep, :
                ].astype(bf16)

    scores = mm(xm[...], fhi[...]) + mm(xm[...], flo[...])
    line = iota((out_x * deep, 1), 0)
    line_x, line_z = line // deep, line % deep
    good = (
        ((line_z > 0) | (me_d > 0))
        & ((line_z <= zc_rows) | (me_d == 0))
        & ((line_x > 0) | (me_s > 0))
        & ((line_x < out_x - 1) | (me_s < shots - 1))
    )
    response = jnp.where(good, scores / (1.0 + scores * scores), 0.0)
    res_hi, res_lo = split(response, 2)

    def nt(a, b):
        return lax.dot_general(a, b, NT, preferred_element_type=f32)

    sb[...] = nt(res_hi, fhi[...]) + nt(res_lo, fhi[...]) + nt(res_hi, flo[...])

    for k in range(1, shots):
        from_s = lax.rem(me_s + shots - k, shots)
        term_copy(k, from_s, peer(k)).wait_recv()
    for q in range(tiles):
        sides = []
        for i in range(2):
            x = 2 * q + i
            value = None
            for a in (-1, 0, 1):
                for b in (-1, 0, 1):
                    ab = 3 * (a + 1) + b + 1
                    piece = sb[
                        pl.ds((x + 1 - b) * deep + 1 - a, zc_rows), ab * wy : (ab + 1) * wy
                    ]
                    value = piece if value is None else value + piece
            sides.append(value)
        total = terms[pl.ds(pl.multiple_of(me_s * block, 8) + q * zc_rows, zc_rows), :]
        for k in range(1, shots):
            total = total + arrived[
                lax.rem(me_s + shots - k, shots), q * zc_rows : (q + 1) * zc_rows, :
            ]
        cut = slice(q * wy, (q + 1) * wy)
        scale = -2.0 * courant * courant / cv[:, cut]
        grad[:, cut] = total * scale + jnp.where(left, sides[0], sides[1])
    t_copy.wait_recv()
    traces[0] = tr_own[:steps] + tr_other[:steps]

    for k in range(1, shots):
        vel_copy(k, me_s, peer(k)).wait_send()
        term_copy(k, me_s, peer(k)).wait_send()
    for c in sent:
        c.wait_send()
    w_copy.wait_send()
    t_copy.wait_send()
    for c in stores:
        c.wait()


def body(
    shots, wave_prev, wave_now, adjoint, coarse_velocity, filters, wavelet, source_cell,
    receiver_cells,
):
    _, steps, rows, wx, wy = adjoint.shape
    zc_rows, ncol = coarse_velocity.shape
    half_y = wy // 2
    tiles = ncol // wy
    pairs_x = shots * tiles
    chans = filters.shape[0]
    count = receiver_cells.shape[1]
    out_x, deep = 2 * tiles + 2, 2 * zc_rows
    vmem = pl.BlockSpec(memory_space=pltpu.VMEM)
    smem = pl.BlockSpec(memory_space=pltpu.SMEM)
    anyw = pl.BlockSpec(memory_space=pl.ANY)
    trace_rows = -(-steps // 8) * 8
    dma = pltpu.SemaphoreType.DMA
    field = pltpu.VMEM((rows + 2 * HALO, wx, wy), f32)
    scratch = (
        [field] * (steps + 2)
        + [pltpu.VMEM((rows, wx, wy), f32)] * steps
        + [
            pltpu.VMEM((zc_rows, wx, wy), f32),
            pltpu.VMEM((zc_rows, wx, wy), f32),
            pltpu.VMEM((wx, 3 * wx), bf16),
            pltpu.VMEM((3 * wy, wy), bf16),
            pltpu.VMEM((2, wx, wy), f32),
            pltpu.VMEM((shots, zc_rows, ncol), f32),
            pltpu.VMEM((2, pairs_x * zc_rows, wy), f32),
            pltpu.VMEM((tiles + 2, zc_rows, wy), f32),
            pltpu.VMEM((tiles + 2, zc_rows, wy), f32),
            pltpu.VMEM((2 * tiles + 4, 3 * zc_rows, wy), f32),
            pltpu.VMEM((out_x * deep, 9 * wy), bf16),
            pltpu.VMEM((9 * wy, chans * half_y), bf16),
            pltpu.VMEM((9 * wy, chans * half_y), bf16),
            pltpu.VMEM((out_x * deep, 9 * wy), f32),
            pltpu.VMEM((wx, wy), f32),
            pltpu.VMEM((pairs_x * zc_rows, wy), f32),
            pltpu.VMEM((shots, tiles * zc_rows, wy), f32),
            pltpu.VMEM((steps, count, wy), f32),
            pltpu.VMEM((trace_rows, count), f32),
            pltpu.VMEM((trace_rows, count), f32),
            dma((2 + steps,)),
            dma((2,)),
            dma((steps,)),
            dma((steps,)),
            dma((shots,)),
            dma((shots,)),
            dma((shots,)),
            dma((shots,)),
            dma((2,)),
            dma((2,)),
        ]
    )
    return pl.pallas_call(
        functools.partial(kernel, shots, steps),
        out_shape=(
            jax.ShapeDtypeStruct((zc_rows, ncol), f32),
            jax.ShapeDtypeStruct(wave_prev.shape, f32),
            jax.ShapeDtypeStruct(wave_now.shape, f32),
            jax.ShapeDtypeStruct((1, steps, count), f32),
        ),
        in_specs=[anyw, anyw, anyw, vmem, vmem, smem, smem, smem, vmem],
        out_specs=(vmem, anyw, anyw, vmem),
        scratch_shapes=scratch,
        compiler_params=pltpu.CompilerParams(
            collective_id=0, has_side_effects=True, vmem_limit_bytes=52 * 2**20
        ),
    )(
        wave_prev, wave_now, adjoint, coarse_velocity, filters, wavelet, source_cell,
        receiver_cells, receiver_cells,
    )


def solution(mesh):
    return jax.shard_map(
        functools.partial(body, mesh.shape["shot"]),
        mesh=mesh,
        in_specs=(
            P(("grp", "shot"), "depth", None, None),
            P(("grp", "shot"), "depth", None, None),
            P(("grp", "shot"), None, "depth", None, None),
            P(("grp", "depth"), "shot"),
            P(),
            P(("grp", "shot"), None),
            P(("grp", "shot")),
            P(("grp", "shot"), None),
        ),
        out_specs=(
            P(("grp", "depth"), "shot"),
            P(("grp", "shot"), "depth", None, None),
            P(("grp", "shot"), "depth", None, None),
            P(("grp", "shot"), None, None),
        ),
        check_vma=False,
    )
```

```python
import functools

import jax
import jax.numpy as jnp
from jax import lax
from jax.experimental import pallas as pl
from jax.experimental.pallas import tpu as pltpu
from jax.sharding import PartitionSpec as P

coeffs = (-205.0 / 72.0, 8.0 / 5.0, -1.0 / 5.0, 8.0 / 315.0, -1.0 / 560.0)
courant = 0.1
HALO = 4
GRANT = 56 * 2**20
f32, bf16, i32 = jnp.float32, jnp.bfloat16, jnp.int32
NT = (((1,), (1,)), ((), ()))
TN = (((0,), (0,)), ((), ()))


def iota(shape, dim):
    return lax.broadcasted_iota(i32, shape, dim)


def split(value, parts):
    out = []
    for _ in range(parts - 1):
        part = value.astype(bf16)
        value = value - part.astype(f32)
        out.append(part)
    return out + [value.astype(bf16)]


def mm(a, b):
    return jnp.dot(a, b, preferred_element_type=f32)


def kernel(
    shots, steps,
    prev_hbm, now_hbm, adj_hbm, cv_hbm, filt_hbm, wav_hbm, src, rec_hbm,
    grad, pout, nout, traces,
    *scratch,
):
    fields = scratch[: steps + 2]
    adjs = scratch[steps + 2 : 2 * steps + 2]
    (
        cv, filt, wav, rec_s, rec_v, speed, acc, bx, by, lat, vel, velf, wown, wother, zx, xm, fhi, flo, sb,
        tmp, terms, arrived, picked, tr_own, tr_other,
        in_sem, out_sem, h_send, h_recv, v_send, v_recv, r_send, r_recv, w_sem, t_sem,
    ) = scratch[2 * steps + 2 :]
    rows, wx, wy = adjs[0].shape
    zc_rows, ncol = cv.shape
    half_y = wy // 2
    tiles = ncol // wy
    pairs_x = shots * tiles
    chans = filt.shape[0]
    me_s, me_d = lax.axis_index("shot"), lax.axis_index("depth")
    other = {"depth": 1 - me_d}
    MESH = pl.DeviceIdType.MESH

    def peer(k):
        return lax.rem(me_s + k, shots)

    load_now = pltpu.make_async_copy(now_hbm.at[0], fields[1].at[pl.ds(HALO, rows)], in_sem.at[0])
    load_prev = pltpu.make_async_copy(prev_hbm.at[0], fields[0].at[pl.ds(HALO, rows)], in_sem.at[1])
    load_adj = [
        pltpu.make_async_copy(adj_hbm.at[0, t], adjs[t], in_sem.at[2 + t]) for t in range(steps)
    ]
    small = [
        pltpu.make_async_copy(a, b, in_sem.at[2 + steps + n])
        for n, (a, b) in enumerate(
            ((cv_hbm, cv), (filt_hbm, filt), (wav_hbm, wav), (rec_hbm, rec_s), (rec_hbm, rec_v))
        )
    ]
    for c in small:
        c.start()
    load_now.start()
    load_prev.start()
    for c in load_adj:
        c.start()

    barrier = pltpu.get_barrier_semaphore()
    for k in range(1, shots):
        pl.semaphore_signal(barrier, inc=1, device_id={"shot": peer(k)}, device_id_type=MESH)
    pl.semaphore_signal(barrier, inc=1, device_id=other, device_id_type=MESH)
    small[0].wait()
    pl.semaphore_wait(barrier, shots)

    def vel_copy(k, slot, to):
        return pltpu.make_async_remote_copy(
            src_ref=cv, dst_ref=vel.at[slot], send_sem=v_send.at[k], recv_sem=v_recv.at[k],
            device_id={"shot": to}, device_id_type=MESH,
        )

    for k in range(1, shots):
        vel_copy(k, me_s, peer(k)).start()
    inner = jnp.where(me_d == 0, rows - HALO, 0)
    far = jnp.where(me_d == 0, 0, rows + HALO)
    first_halo = pltpu.make_async_remote_copy(
        src_ref=now_hbm.at[0, pl.ds(inner, HALO)], dst_ref=fields[1].at[pl.ds(far, HALO)],
        send_sem=h_send.at[0], recv_sem=h_recv.at[0], device_id=other, device_id_type=MESH,
    )
    first_halo.start()

    for c in small[1:]:
        c.wait()
    for t in range(steps):
        fields[t + 1][pl.ds(far, HALO)] = jnp.zeros((HALO, wx, wy), f32)
    gap_x = jnp.abs(iota((wx, wx), 0) - iota((wx, wx), 1))
    gap_y = jnp.abs(iota((wy, wy), 0) - iota((wy, wy), 1))

    def band(gap):
        value = jnp.where(gap == 0, 1.5 * coeffs[0], 0.0).astype(f32)
        for k in range(1, 5):
            value = jnp.where(gap == k, coeffs[k], value)
        return split(value, 2)

    high, low = band(gap_x)
    bx[...] = jnp.concatenate([high, high, low], axis=1)
    high, low = band(gap_y)
    by[...] = jnp.concatenate([high, high, low], axis=0)

    width = chans * half_y
    spread = (iota((chans, width), 1) // half_y == iota((chans, width), 0)).astype(f32)
    taps = lax.dot_general(
        filt[...], spread, TN, precision=lax.Precision.HIGHEST, preferred_element_type=f32
    )
    taps_hi = taps.astype(bf16).astype(f32)
    taps_lo = taps - taps_hi
    shift_y = iota((half_y, width), 0) - iota((half_y, width), 1) % half_y
    for ab in range(9):
        for weights, out in ((taps_hi, fhi), (taps_lo, flo)):
            value = jnp.zeros((half_y, width), f32)
            for e in (-1, 0, 1):
                value = jnp.where(shift_y == e, weights[3 * ab + e + 1 : 3 * ab + e + 2], value)
            value = value.astype(bf16)
            out[pl.ds(ab * wy, half_y), :] = value
            out[pl.ds(ab * wy + half_y, half_y), :] = value

    hit = src[0]
    hit_z = hit // (wx * wy) - me_d * rows
    hit_x = hit // wy % wx
    hit_y = hit % wy
    spot = ((iota((wx, wy), 0) == hit_x) & (iota((wx, wy), 1) == hit_y)).astype(f32)
    tmp[...] = spot
    chunk = 32

    def pair(t, zc):
        current, earlier, following = fields[t + 1], fields[t], fields[t + 2]
        z0 = 2 * zc
        halves = [split(current[z0 + HALO + i], 2) for i in range(2)]
        wide = [jnp.concatenate([halves[0][h], halves[1][h]], axis=1) for h in range(2)]
        tall = [jnp.concatenate([halves[0][h], halves[1][h]], axis=0) for h in range(2)]
        along_x = mm(bx[...], jnp.concatenate([wide[0], wide[1], wide[0]], axis=0))
        along_y = mm(jnp.concatenate([tall[0], tall[1], tall[0]], axis=1), by[...])
        for i in range(2):
            lat[i] = along_x[:, i * wy : (i + 1) * wy] + along_y[i * wx : (i + 1) * wx]
        for r in range(0, wx, chunk):
            cut = pl.ds(r, chunk)
            speed_cut = None if t == 0 else speed[zc, cut, :]
            spot_cut = tmp[cut, :]
            image = None
            planes = [current[z0 + k, cut, :] for k in range(2 * HALO + 2)]
            for i in range(2):
                pulse = jnp.where(hit_z == z0 + i, wav[0, t], 0.0)
                lap = lat[i, cut, :] + spot_cut * pulse
                for k in range(1, 5):
                    lap = lap + coeffs[k] * (planes[i + HALO + k] + planes[i + HALO - k])
                if t == 0:
                    following[z0 + i + HALO, cut, :] = lap
                else:
                    following[z0 + i + HALO, cut, :] = (
                        2.0 * planes[i + HALO] - earlier[z0 + i + HALO, cut, :] + speed_cut * lap
                    )
                term = adjs[t][z0 + i, cut, :] * lap
                image = term if image is None else image + term
            if t == 0:
                acc[zc, cut, :] = image
            else:
                acc[zc, cut, :] = acc[zc, cut, :] + image

    def finish(zc):
        for i in range(2):
            z = 2 * zc + i + HALO
            for r in range(0, wx, chunk):
                cut = pl.ds(r, chunk)
                fields[2][z, cut, :] = (
                    2.0 * fields[1][z, cut, :]
                    - fields[0][z, cut, :]
                    + speed[zc, cut, :] * fields[2][z, cut, :]
                )

    edge_pairs = HALO // 2
    inside_pairs = rows // 2 - edge_pairs
    inside_first = me_d * edge_pairs
    edge_first = jnp.where(me_d == 0, inside_pairs, 0)
    sent = [first_halo]

    def send_edge(t):
        copy = pltpu.make_async_remote_copy(
            src_ref=fields[t + 1].at[pl.ds(inner + HALO, HALO)],
            dst_ref=fields[t + 1].at[pl.ds(far, HALO)],
            send_sem=h_send.at[t], recv_sem=h_recv.at[t],
            device_id=other, device_id_type=MESH,
        )
        copy.start()
        sent.append(copy)

    load_now.wait()
    load_adj[0].wait()

    @pl.loop(0, inside_pairs)
    def _(i):
        pair(0, inside_first + i)

    first_halo.wait_recv()

    @pl.loop(0, edge_pairs)
    def _(i):
        pair(0, edge_first + i)

    load_prev.wait()
    vel[pl.ds(me_s, 1)] = cv[...][None]
    for k in range(1, shots):
        from_s = lax.rem(me_s + shots - k, shots)
        vel_copy(k, from_s, peer(k)).wait_recv()
    stacked = jnp.concatenate(
        [vel[s, :, q * wy : (q + 1) * wy] for s in range(shots) for q in range(tiles)], axis=0
    )
    up_row, up_col = iota((wy, 2 * wy), 0), iota((wy, 2 * wy), 1)
    up = (up_row == up_col // wy * half_y + up_col % wy // 2).astype(f32).astype(bf16)
    fine = mm(
        jnp.concatenate(split(stacked, 3), axis=1), jnp.concatenate([up, up, up], axis=0)
    )
    velf[0] = fine[:, :wy]
    velf[1] = fine[:, wy:]
    for z in range(zc_rows):
        for i in range(2):
            plane = courant * velf[i, pl.ds(z, pairs_x, stride=zc_rows), :]
            plane = plane * plane
            for j in range(2):
                speed[z, pl.ds(2 * i + j, pairs_x, stride=4), :] = plane

    before = vel[jnp.maximum(me_s - 1, 0), :, ncol - wy :]
    after = vel[jnp.minimum(me_s + 1, shots - 1), :, :wy]
    wown[0] = jnp.where(me_s > 0, before, 0.0)
    for q in range(tiles):
        wown[q + 1] = cv[:, q * wy : (q + 1) * wy]
    wown[tiles + 1] = jnp.where(me_s < shots - 1, after, 0.0)
    w_copy = pltpu.make_async_remote_copy(
        src_ref=wown, dst_ref=wother, send_sem=w_sem.at[0], recv_sem=w_sem.at[1],
        device_id=other, device_id_type=MESH,
    )
    w_copy.start()

    @pl.loop(0, edge_pairs)
    def _(i):
        finish(edge_first + i)

    if steps > 1:
        send_edge(1)

    @pl.loop(0, inside_pairs)
    def _(i):
        finish(inside_first + i)

    stores = []
    for t in range(steps):
        if t > 0:
            load_adj[t].wait()

            @pl.loop(0, inside_pairs)
            def _(i):
                pair(t, inside_first + i)

            sent[t].wait_recv()

            @pl.loop(0, edge_pairs)
            def _(i):
                pair(t, edge_first + i)

            if t + 1 < steps:
                send_edge(t + 1)
        if t + 2 >= steps:
            out = pout if t + 2 == steps else nout
            store = pltpu.make_async_copy(
                fields[t + 2].at[pl.ds(HALO, rows)], out.at[0], out_sem.at[t + 2 - steps]
            )
            store.start()
            stores.append(store)

    fold_row, fold_col = iota((wy, wy), 0), iota((wy, wy), 1)
    fold = (fold_row // 2 == fold_col % half_y).astype(f32).astype(bf16)
    fold = jnp.concatenate([fold, fold], axis=0)
    left = iota((1, wy), 1) < half_y
    for z in range(zc_rows):
        fields[0][z] = mm(jnp.concatenate(split(acc[z], 2), axis=1), fold)
    for z in range(zc_rows):
        quarter = [fields[0][z, pl.ds(j, pairs_x, stride=4), :] for j in range(4)]
        terms[pl.ds(z, pairs_x, stride=zc_rows), :] = jnp.where(
            left, quarter[0] + quarter[1], quarter[2] + quarter[3]
        )
    block = tiles * zc_rows

    def term_copy(k, slot, to):
        return pltpu.make_async_remote_copy(
            src_ref=terms.at[pl.ds(pl.multiple_of(to * block, 8), block)],
            dst_ref=arrived.at[slot], send_sem=r_send.at[k], recv_sem=r_recv.at[k],
            device_id={"shot": to}, device_id_type=MESH,
        )

    for k in range(1, shots):
        term_copy(k, me_s, peer(k)).start()

    plane_size = wx * wy
    top = rows * plane_size - 1

    @pl.loop(0, rec_s.shape[1])
    def _(r):
        cell = jnp.clip(rec_s[0, r] - me_d * rows * plane_size, 0, top)
        z, x = cell // plane_size, cell // wy % wx
        for t in range(steps):
            picked[t, pl.ds(r, 1), :] = fields[t + 2][z + HALO, pl.ds(x, 1), :]

    cells = rec_v[...] - me_d * rows * plane_size
    inside = (cells >= 0) & (cells <= top)
    count = rec_s.shape[1]
    lane_hit = (iota((wy, count), 0) == jnp.clip(cells, 0, top) % wy) & inside
    tr_own[...] = jnp.zeros_like(tr_own)
    for t in range(steps):
        flipped = jnp.where(lane_hit, picked[t].T, 0.0)
        tr_own[pl.ds(t, 1), :] = jnp.sum(flipped, axis=0, keepdims=True)
    t_copy = pltpu.make_async_remote_copy(
        src_ref=tr_own, dst_ref=tr_other, send_sem=t_sem.at[0], recv_sem=t_sem.at[1],
        device_id=other, device_id_type=MESH,
    )
    t_copy.start()

    w_copy.wait_recv()
    for g in range(tiles + 2):
        own, near = wown[g], wother[g]
        tall = jnp.concatenate(
            [jnp.where(me_d == 0, 0.0, near), own, jnp.where(me_d == 0, near, 0.0)], axis=0
        )
        turned = pltpu.roll(tall, half_y, axis=1)
        for i, both in enumerate((jnp.where(left, tall, turned), jnp.where(left, turned, tall))):
            part = both.astype(bf16).astype(f32)
            zx[2 * g + i] = jnp.where(left, part, both - part)
    out_x = 2 * tiles + 2
    deep = 2 * zc_rows

    @pl.loop(0, out_x)
    def _(j):
        for a in range(3):
            for b in range(3):
                ab = 3 * a + b
                xm[pl.ds(pl.multiple_of(j * deep, 16), deep), ab * wy : (ab + 1) * wy] = zx[
                    j + b, zc_rows - 2 + a : zc_rows - 2 + a + deep, :
                ].astype(bf16)

    scores = mm(xm[...], fhi[...]) + mm(xm[...], flo[...])
    line = iota((out_x * deep, 1), 0)
    line_x, line_z = line // deep, line % deep
    good = (
        ((line_z > 0) | (me_d > 0))
        & ((line_z <= zc_rows) | (me_d == 0))
        & ((line_x > 0) | (me_s > 0))
        & ((line_x < out_x - 1) | (me_s < shots - 1))
    )
    response = jnp.where(good, scores / (1.0 + scores * scores), 0.0)
    res_hi, res_lo = split(response, 2)

    def nt(a, b):
        return lax.dot_general(a, b, NT, preferred_element_type=f32)

    sb[...] = nt(res_hi, fhi[...]) + nt(res_lo, fhi[...]) + nt(res_hi, flo[...])

    for k in range(1, shots):
        from_s = lax.rem(me_s + shots - k, shots)
        term_copy(k, from_s, peer(k)).wait_recv()
    for q in range(tiles):
        sides = []
        for i in range(2):
            x = 2 * q + i
            value = None
            for a in (-1, 0, 1):
                for b in (-1, 0, 1):
                    ab = 3 * (a + 1) + b + 1
                    piece = sb[
                        pl.ds((x + 1 - b) * deep + 1 - a, zc_rows), ab * wy : (ab + 1) * wy
                    ]
                    value = piece if value is None else value + piece
            sides.append(value)
        total = terms[pl.ds(pl.multiple_of(me_s * block, 8) + q * zc_rows, zc_rows), :]
        for k in range(1, shots):
            total = total + arrived[
                lax.rem(me_s + shots - k, shots), q * zc_rows : (q + 1) * zc_rows, :
            ]
        cut = slice(q * wy, (q + 1) * wy)
        scale = -2.0 * courant * courant / cv[:, cut]
        grad[:, cut] = total * scale + jnp.where(left, sides[0], sides[1])
    t_copy.wait_recv()
    traces[0] = tr_own[:steps] + tr_other[:steps]

    for k in range(1, shots):
        vel_copy(k, me_s, peer(k)).wait_send()
        term_copy(k, me_s, peer(k)).wait_send()
    for c in sent:
        c.wait_send()
    w_copy.wait_send()
    t_copy.wait_send()
    for c in stores:
        c.wait()


def store_kernel(*refs):
    ins, outs, stages = refs[:4], refs[4:8], refs[8:12]
    sem_in, sem_out = refs[12:]
    loads, stores = [], []
    for n in (1, 2, 0, 3):
        rows = ins[n].shape[1]
        pieces = 4 if n in (1, 2) and rows % 4 == 0 else 1
        for c in range(pieces):
            if n == 0:
                parts = [ref for ref in (ins[n], stages[n], outs[n])]
            else:
                cut = pl.ds(c * (rows // pieces), rows // pieces)
                parts = [ref.at[:, cut] for ref in (ins[n], stages[n], outs[n])]
            loads.append(pltpu.make_async_copy(parts[0], parts[1], sem_in.at[n, c]))
            stores.append(pltpu.make_async_copy(parts[1], parts[2], sem_out.at[n, c]))
    for c in loads:
        c.start()
    for load, store in zip(loads, stores):
        load.wait()
        store.start()
    for c in stores:
        c.wait()


def body(
    shots, wave_prev, wave_now, adjoint, coarse_velocity, filters, wavelet, source_cell,
    receiver_cells,
):
    _, steps, rows, wx, wy = adjoint.shape
    zc_rows, ncol = coarse_velocity.shape
    half_y = wy // 2
    tiles = ncol // wy
    pairs_x = shots * tiles
    chans = filters.shape[0]
    count = receiver_cells.shape[1]
    out_x, deep = 2 * tiles + 2, 2 * zc_rows
    vmem = pl.BlockSpec(memory_space=pltpu.VMEM)
    smem = pl.BlockSpec(memory_space=pltpu.SMEM)
    hbm = pl.BlockSpec(memory_space=pltpu.HBM)
    trace_rows = -(-steps // 8) * 8
    dma = pltpu.SemaphoreType.DMA
    field = pltpu.VMEM((rows + 2 * HALO, wx, wy), f32)
    scratch = (
        [field] * (steps + 2)
        + [pltpu.VMEM((rows, wx, wy), f32)] * steps
        + [
            pltpu.VMEM((zc_rows, ncol), f32),
            pltpu.VMEM(filters.shape, f32),
            pltpu.SMEM(wavelet.shape, f32),
            pltpu.SMEM(receiver_cells.shape, i32),
            pltpu.VMEM(receiver_cells.shape, i32),
            pltpu.VMEM((zc_rows, wx, wy), f32),
            pltpu.VMEM((zc_rows, wx, wy), f32),
            pltpu.VMEM((wx, 3 * wx), bf16),
            pltpu.VMEM((3 * wy, wy), bf16),
            pltpu.VMEM((2, wx, wy), f32),
            pltpu.VMEM((shots, zc_rows, ncol), f32),
            pltpu.VMEM((2, pairs_x * zc_rows, wy), f32),
            pltpu.VMEM((tiles + 2, zc_rows, wy), f32),
            pltpu.VMEM((tiles + 2, zc_rows, wy), f32),
            pltpu.VMEM((2 * tiles + 4, 3 * zc_rows, wy), f32),
            pltpu.VMEM((out_x * deep, 9 * wy), bf16),
            pltpu.VMEM((9 * wy, chans * half_y), bf16),
            pltpu.VMEM((9 * wy, chans * half_y), bf16),
            pltpu.VMEM((out_x * deep, 9 * wy), f32),
            pltpu.VMEM((wx, wy), f32),
            pltpu.VMEM((pairs_x * zc_rows, wy), f32),
            pltpu.VMEM((shots, tiles * zc_rows, wy), f32),
            pltpu.VMEM((steps, count, wy), f32),
            pltpu.VMEM((trace_rows, count), f32),
            pltpu.VMEM((trace_rows, count), f32),
            dma((7 + steps,)),
            dma((2,)),
            dma((steps,)),
            dma((steps,)),
            dma((shots,)),
            dma((shots,)),
            dma((shots,)),
            dma((shots,)),
            dma((2,)),
            dma((2,)),
        ]
    )
    out_shape = (
        jax.ShapeDtypeStruct((zc_rows, ncol), f32),
        jax.ShapeDtypeStruct(wave_prev.shape, f32),
        jax.ShapeDtypeStruct(wave_now.shape, f32),
        jax.ShapeDtypeStruct((1, steps, count), f32),
    )
    results = pl.pallas_call(
        functools.partial(kernel, shots, steps),
        out_shape=out_shape,
        in_specs=[hbm, hbm, hbm, hbm, hbm, hbm, smem, hbm],
        out_specs=(vmem, hbm, hbm, vmem),
        scratch_shapes=scratch,
        compiler_params=pltpu.CompilerParams(
            collective_id=0, has_side_effects=True, vmem_limit_bytes=GRANT
        ),
    )(
        wave_prev, wave_now, adjoint, coarse_velocity, filters, wavelet, source_cell,
        receiver_cells,
    )
    return pl.pallas_call(
        store_kernel,
        out_shape=out_shape,
        in_specs=[hbm] * 4,
        out_specs=(hbm,) * 4,
        scratch_shapes=[pltpu.VMEM(x.shape, f32) for x in out_shape] + [dma((4, 4)), dma((4, 4))],
        compiler_params=pltpu.CompilerParams(vmem_limit_bytes=GRANT),
    )(*results)


def solution(mesh):
    return jax.shard_map(
        functools.partial(body, mesh.shape["shot"]),
        mesh=mesh,
        in_specs=(
            P(("grp", "shot"), "depth", None, None),
            P(("grp", "shot"), "depth", None, None),
            P(("grp", "shot"), None, "depth", None, None),
            P(("grp", "depth"), "shot"),
            P(),
            P(("grp", "shot"), None),
            P(("grp", "shot")),
            P(("grp", "shot"), None),
        ),
        out_specs=(
            P(("grp", "depth"), "shot"),
            P(("grp", "shot"), "depth", None, None),
            P(("grp", "shot"), "depth", None, None),
            P(("grp", "shot"), None, None),
        ),
        check_vma=False,
    )
```

```python
import functools

import jax
import jax.numpy as jnp
from jax import lax
from jax.experimental import pallas as pl
from jax.experimental.pallas import tpu as pltpu
from jax.sharding import PartitionSpec as P

coeffs = (-205.0 / 72.0, 8.0 / 5.0, -1.0 / 5.0, 8.0 / 315.0, -1.0 / 560.0)
courant = 0.1
HALO = 4
GRANT = 56 * 2**20
f32, bf16, i32 = jnp.float32, jnp.bfloat16, jnp.int32
NT = (((1,), (1,)), ((), ()))
TN = (((0,), (0,)), ((), ()))


def iota(shape, dim):
    return lax.broadcasted_iota(i32, shape, dim)


def split(value, parts):
    out = []
    for _ in range(parts - 1):
        part = value.astype(bf16)
        value = value - part.astype(f32)
        out.append(part)
    return out + [value.astype(bf16)]


def mm(a, b):
    return jnp.dot(a, b, preferred_element_type=f32)


def kernel(
    shots, steps,
    prev_hbm, now_hbm, adj_hbm, cv_hbm, filt_hbm, wav_hbm, src, rec_hbm,
    grad, pout, nout, traces,
    *scratch,
):
    fields = scratch[: steps + 2]
    adjs = scratch[steps + 2 : 2 * steps + 2]
    (
        cv, filt, wav, rec_s, rec_v, speed, acc, bx, by, lat, vel, velf, wown, wother, zx, xm, fhi, flo, sb,
        tmp, terms, arrived, picked, tr_own, tr_other,
        in_sem, out_sem, h_send, h_recv, v_send, v_recv, r_send, r_recv, w_sem, t_sem,
    ) = scratch[2 * steps + 2 :]
    rows, wx, wy = adjs[0].shape
    zc_rows, ncol = cv.shape
    half_y = wy // 2
    tiles = ncol // wy
    pairs_x = shots * tiles
    chans = filt.shape[0]
    me_s, me_d = lax.axis_index("shot"), lax.axis_index("depth")
    other = {"depth": 1 - me_d}
    MESH = pl.DeviceIdType.MESH

    def peer(k):
        return lax.rem(me_s + k, shots)

    load_now = pltpu.make_async_copy(now_hbm.at[0], fields[1].at[pl.ds(HALO, rows)], in_sem.at[0])
    load_prev = pltpu.make_async_copy(prev_hbm.at[0], fields[0].at[pl.ds(HALO, rows)], in_sem.at[1])
    load_adj = [
        pltpu.make_async_copy(adj_hbm.at[0, t], adjs[t], in_sem.at[2 + t]) for t in range(steps)
    ]
    small = [
        pltpu.make_async_copy(a, b, in_sem.at[2 + steps + n])
        for n, (a, b) in enumerate(
            ((cv_hbm, cv), (filt_hbm, filt), (wav_hbm, wav), (rec_hbm, rec_s), (rec_hbm, rec_v))
        )
    ]
    for c in small:
        c.start()
    load_now.start()
    load_prev.start()
    for c in load_adj:
        c.start()

    barrier = pltpu.get_barrier_semaphore()
    for k in range(1, shots):
        pl.semaphore_signal(barrier, inc=1, device_id={"shot": peer(k)}, device_id_type=MESH)
    pl.semaphore_signal(barrier, inc=1, device_id=other, device_id_type=MESH)
    small[0].wait()
    pl.semaphore_wait(barrier, shots)

    def vel_copy(k, slot, to):
        return pltpu.make_async_remote_copy(
            src_ref=cv, dst_ref=vel.at[slot], send_sem=v_send.at[k], recv_sem=v_recv.at[k],
            device_id={"shot": to}, device_id_type=MESH,
        )

    for k in range(1, shots):
        vel_copy(k, me_s, peer(k)).start()
    inner = jnp.where(me_d == 0, rows - HALO, 0)
    far = jnp.where(me_d == 0, 0, rows + HALO)
    first_halo = pltpu.make_async_remote_copy(
        src_ref=now_hbm.at[0, pl.ds(inner, HALO)], dst_ref=fields[1].at[pl.ds(far, HALO)],
        send_sem=h_send.at[0], recv_sem=h_recv.at[0], device_id=other, device_id_type=MESH,
    )
    first_halo.start()

    for c in small[1:]:
        c.wait()
    for t in range(steps):
        fields[t + 1][pl.ds(far, HALO)] = jnp.zeros((HALO, wx, wy), f32)
    gap_x = jnp.abs(iota((wx, wx), 0) - iota((wx, wx), 1))
    gap_y = jnp.abs(iota((wy, wy), 0) - iota((wy, wy), 1))

    def band(gap):
        value = jnp.where(gap == 0, 1.5 * coeffs[0], 0.0).astype(f32)
        for k in range(1, 5):
            value = jnp.where(gap == k, coeffs[k], value)
        return split(value, 2)

    high, low = band(gap_x)
    bx[...] = jnp.concatenate([high, high, low], axis=1)
    high, low = band(gap_y)
    by[...] = jnp.concatenate([high, high, low], axis=0)

    width = chans * half_y
    spread = (iota((chans, width), 1) // half_y == iota((chans, width), 0)).astype(f32)
    taps = lax.dot_general(
        filt[...], spread, TN, precision=lax.Precision.HIGHEST, preferred_element_type=f32
    )
    taps_hi = taps.astype(bf16).astype(f32)
    taps_lo = taps - taps_hi
    shift_y = iota((half_y, width), 0) - iota((half_y, width), 1) % half_y
    for ab in range(9):
        for weights, out in ((taps_hi, fhi), (taps_lo, flo)):
            value = jnp.zeros((half_y, width), f32)
            for e in (-1, 0, 1):
                value = jnp.where(shift_y == e, weights[3 * ab + e + 1 : 3 * ab + e + 2], value)
            value = value.astype(bf16)
            out[pl.ds(ab * wy, half_y), :] = value
            out[pl.ds(ab * wy + half_y, half_y), :] = value

    hit = src[0]
    hit_z = hit // (wx * wy) - me_d * rows
    hit_x = hit // wy % wx
    hit_y = hit % wy
    spot = ((iota((wx, wy), 0) == hit_x) & (iota((wx, wy), 1) == hit_y)).astype(f32)
    tmp[...] = spot
    chunk = 32

    def pairs(t, first, count):
        together = 2 if count % 2 == 0 else 1

        @pl.loop(0, count // together)
        def _(i):
            for u in range(together):
                pair(t, first + i * together + u, 2 * u)

    def pair(t, zc, slot):
        current, earlier, following = fields[t + 1], fields[t], fields[t + 2]
        z0 = 2 * zc
        halves = [split(current[z0 + HALO + i], 2) for i in range(2)]
        wide = [jnp.concatenate([halves[0][h], halves[1][h]], axis=1) for h in range(2)]
        tall = [jnp.concatenate([halves[0][h], halves[1][h]], axis=0) for h in range(2)]
        along_x = mm(bx[...], jnp.concatenate([wide[0], wide[1], wide[0]], axis=0))
        along_y = mm(jnp.concatenate([tall[0], tall[1], tall[0]], axis=1), by[...])
        for i in range(2):
            lat[slot + i] = along_x[:, i * wy : (i + 1) * wy] + along_y[i * wx : (i + 1) * wx]
        for r in range(0, wx, chunk):
            cut = pl.ds(r, chunk)
            speed_cut = None if t == 0 else speed[zc, cut, :]
            spot_cut = tmp[cut, :]
            image = None
            planes = [current[z0 + k, cut, :] for k in range(2 * HALO + 2)]
            for i in range(2):
                pulse = jnp.where(hit_z == z0 + i, wav[0, t], 0.0)
                lap = lat[slot + i, cut, :] + spot_cut * pulse
                for k in range(1, 5):
                    lap = lap + coeffs[k] * (planes[i + HALO + k] + planes[i + HALO - k])
                if t == 0:
                    following[z0 + i + HALO, cut, :] = lap
                else:
                    following[z0 + i + HALO, cut, :] = (
                        2.0 * planes[i + HALO] - earlier[z0 + i + HALO, cut, :] + speed_cut * lap
                    )
                term = adjs[t][z0 + i, cut, :] * lap
                image = term if image is None else image + term
            if t == 0:
                acc[zc, cut, :] = image
            else:
                acc[zc, cut, :] = acc[zc, cut, :] + image

    def finish(zc):
        for i in range(2):
            z = 2 * zc + i + HALO
            for r in range(0, wx, chunk):
                cut = pl.ds(r, chunk)
                fields[2][z, cut, :] = (
                    2.0 * fields[1][z, cut, :]
                    - fields[0][z, cut, :]
                    + speed[zc, cut, :] * fields[2][z, cut, :]
                )

    edge_pairs = HALO // 2
    inside_pairs = rows // 2 - edge_pairs
    inside_first = me_d * edge_pairs
    edge_first = jnp.where(me_d == 0, inside_pairs, 0)
    sent = [first_halo]

    def send_edge(t):
        copy = pltpu.make_async_remote_copy(
            src_ref=fields[t + 1].at[pl.ds(inner + HALO, HALO)],
            dst_ref=fields[t + 1].at[pl.ds(far, HALO)],
            send_sem=h_send.at[t], recv_sem=h_recv.at[t],
            device_id=other, device_id_type=MESH,
        )
        copy.start()
        sent.append(copy)

    load_now.wait()
    load_adj[0].wait()

    pairs(0, inside_first, inside_pairs)

    first_halo.wait_recv()

    pairs(0, edge_first, edge_pairs)

    load_prev.wait()
    vel[pl.ds(me_s, 1)] = cv[...][None]
    for k in range(1, shots):
        from_s = lax.rem(me_s + shots - k, shots)
        vel_copy(k, from_s, peer(k)).wait_recv()
    stacked = jnp.concatenate(
        [vel[s, :, q * wy : (q + 1) * wy] for s in range(shots) for q in range(tiles)], axis=0
    )
    up_row, up_col = iota((wy, 2 * wy), 0), iota((wy, 2 * wy), 1)
    up = (up_row == up_col // wy * half_y + up_col % wy // 2).astype(f32).astype(bf16)
    fine = mm(
        jnp.concatenate(split(stacked, 3), axis=1), jnp.concatenate([up, up, up], axis=0)
    )
    velf[0] = fine[:, :wy]
    velf[1] = fine[:, wy:]
    for z in range(zc_rows):
        for i in range(2):
            plane = courant * velf[i, pl.ds(z, pairs_x, stride=zc_rows), :]
            plane = plane * plane
            for j in range(2):
                speed[z, pl.ds(2 * i + j, pairs_x, stride=4), :] = plane

    before = vel[jnp.maximum(me_s - 1, 0), :, ncol - wy :]
    after = vel[jnp.minimum(me_s + 1, shots - 1), :, :wy]
    wown[0] = jnp.where(me_s > 0, before, 0.0)
    for q in range(tiles):
        wown[q + 1] = cv[:, q * wy : (q + 1) * wy]
    wown[tiles + 1] = jnp.where(me_s < shots - 1, after, 0.0)
    w_copy = pltpu.make_async_remote_copy(
        src_ref=wown, dst_ref=wother, send_sem=w_sem.at[0], recv_sem=w_sem.at[1],
        device_id=other, device_id_type=MESH,
    )
    w_copy.start()

    @pl.loop(0, edge_pairs)
    def _(i):
        finish(edge_first + i)

    if steps > 1:
        send_edge(1)

    @pl.loop(0, inside_pairs)
    def _(i):
        finish(inside_first + i)

    stores = []
    for t in range(steps):
        if t > 0:
            load_adj[t].wait()

            pairs(t, inside_first, inside_pairs)

            sent[t].wait_recv()

            pairs(t, edge_first, edge_pairs)

            if t + 1 < steps:
                send_edge(t + 1)
        if t + 2 >= steps:
            out = pout if t + 2 == steps else nout
            store = pltpu.make_async_copy(
                fields[t + 2].at[pl.ds(HALO, rows)], out.at[0], out_sem.at[t + 2 - steps]
            )
            store.start()
            stores.append(store)

    fold_row, fold_col = iota((wy, wy), 0), iota((wy, wy), 1)
    fold = (fold_row // 2 == fold_col % half_y).astype(f32).astype(bf16)
    fold = jnp.concatenate([fold, fold], axis=0)
    left = iota((1, wy), 1) < half_y
    for z in range(zc_rows):
        fields[0][z] = mm(jnp.concatenate(split(acc[z], 2), axis=1), fold)
    for z in range(zc_rows):
        quarter = [fields[0][z, pl.ds(j, pairs_x, stride=4), :] for j in range(4)]
        terms[pl.ds(z, pairs_x, stride=zc_rows), :] = jnp.where(
            left, quarter[0] + quarter[1], quarter[2] + quarter[3]
        )
    block = tiles * zc_rows

    def term_copy(k, slot, to):
        return pltpu.make_async_remote_copy(
            src_ref=terms.at[pl.ds(pl.multiple_of(to * block, 8), block)],
            dst_ref=arrived.at[slot], send_sem=r_send.at[k], recv_sem=r_recv.at[k],
            device_id={"shot": to}, device_id_type=MESH,
        )

    for k in range(1, shots):
        term_copy(k, me_s, peer(k)).start()

    plane_size = wx * wy
    top = rows * plane_size - 1

    @pl.loop(0, rec_s.shape[1])
    def _(r):
        cell = jnp.clip(rec_s[0, r] - me_d * rows * plane_size, 0, top)
        z, x = cell // plane_size, cell // wy % wx
        for t in range(steps):
            picked[t, pl.ds(r, 1), :] = fields[t + 2][z + HALO, pl.ds(x, 1), :]

    cells = rec_v[...] - me_d * rows * plane_size
    inside = (cells >= 0) & (cells <= top)
    count = rec_s.shape[1]
    lane_hit = (iota((wy, count), 0) == jnp.clip(cells, 0, top) % wy) & inside
    tr_own[...] = jnp.zeros_like(tr_own)
    for t in range(steps):
        flipped = jnp.where(lane_hit, picked[t].T, 0.0)
        tr_own[pl.ds(t, 1), :] = jnp.sum(flipped, axis=0, keepdims=True)
    t_copy = pltpu.make_async_remote_copy(
        src_ref=tr_own, dst_ref=tr_other, send_sem=t_sem.at[0], recv_sem=t_sem.at[1],
        device_id=other, device_id_type=MESH,
    )
    t_copy.start()

    w_copy.wait_recv()
    for g in range(tiles + 2):
        own, near = wown[g], wother[g]
        tall = jnp.concatenate(
            [jnp.where(me_d == 0, 0.0, near), own, jnp.where(me_d == 0, near, 0.0)], axis=0
        )
        turned = pltpu.roll(tall, half_y, axis=1)
        for i, both in enumerate((jnp.where(left, tall, turned), jnp.where(left, turned, tall))):
            part = both.astype(bf16).astype(f32)
            zx[2 * g + i] = jnp.where(left, part, both - part)
    out_x = 2 * tiles + 2
    deep = 2 * zc_rows

    @pl.loop(0, out_x)
    def _(j):
        for a in range(3):
            for b in range(3):
                ab = 3 * a + b
                xm[pl.ds(pl.multiple_of(j * deep, 16), deep), ab * wy : (ab + 1) * wy] = zx[
                    j + b, zc_rows - 2 + a : zc_rows - 2 + a + deep, :
                ].astype(bf16)

    scores = mm(xm[...], fhi[...]) + mm(xm[...], flo[...])
    line = iota((out_x * deep, 1), 0)
    line_x, line_z = line // deep, line % deep
    good = (
        ((line_z > 0) | (me_d > 0))
        & ((line_z <= zc_rows) | (me_d == 0))
        & ((line_x > 0) | (me_s > 0))
        & ((line_x < out_x - 1) | (me_s < shots - 1))
    )
    response = jnp.where(good, scores / (1.0 + scores * scores), 0.0)
    res_hi, res_lo = split(response, 2)

    def nt(a, b):
        return lax.dot_general(a, b, NT, preferred_element_type=f32)

    sb[...] = nt(res_hi, fhi[...]) + nt(res_lo, fhi[...]) + nt(res_hi, flo[...])

    for k in range(1, shots):
        from_s = lax.rem(me_s + shots - k, shots)
        term_copy(k, from_s, peer(k)).wait_recv()
    for q in range(tiles):
        sides = []
        for i in range(2):
            x = 2 * q + i
            value = None
            for a in (-1, 0, 1):
                for b in (-1, 0, 1):
                    ab = 3 * (a + 1) + b + 1
                    piece = sb[
                        pl.ds((x + 1 - b) * deep + 1 - a, zc_rows), ab * wy : (ab + 1) * wy
                    ]
                    value = piece if value is None else value + piece
            sides.append(value)
        total = terms[pl.ds(pl.multiple_of(me_s * block, 8) + q * zc_rows, zc_rows), :]
        for k in range(1, shots):
            total = total + arrived[
                lax.rem(me_s + shots - k, shots), q * zc_rows : (q + 1) * zc_rows, :
            ]
        cut = slice(q * wy, (q + 1) * wy)
        scale = -2.0 * courant * courant / cv[:, cut]
        grad[:, cut] = total * scale + jnp.where(left, sides[0], sides[1])
    t_copy.wait_recv()
    traces[0] = tr_own[:steps] + tr_other[:steps]

    for k in range(1, shots):
        vel_copy(k, me_s, peer(k)).wait_send()
        term_copy(k, me_s, peer(k)).wait_send()
    for c in sent:
        c.wait_send()
    w_copy.wait_send()
    t_copy.wait_send()
    for c in stores:
        c.wait()


def store_kernel(*refs):
    ins, outs, stages = refs[:4], refs[4:8], refs[8:12]
    sem_in, sem_out = refs[12:]
    loads, stores = [], []
    for n in (1, 2, 0, 3):
        rows = ins[n].shape[1]
        pieces = 4 if n in (1, 2) and rows % 4 == 0 else 1
        for c in range(pieces):
            if n == 0:
                parts = [ref for ref in (ins[n], stages[n], outs[n])]
            else:
                cut = pl.ds(c * (rows // pieces), rows // pieces)
                parts = [ref.at[:, cut] for ref in (ins[n], stages[n], outs[n])]
            loads.append(pltpu.make_async_copy(parts[0], parts[1], sem_in.at[n, c]))
            stores.append(pltpu.make_async_copy(parts[1], parts[2], sem_out.at[n, c]))
    for c in loads:
        c.start()
    for load, store in zip(loads, stores):
        load.wait()
        store.start()
    for c in stores:
        c.wait()


def body(
    shots, wave_prev, wave_now, adjoint, coarse_velocity, filters, wavelet, source_cell,
    receiver_cells,
):
    _, steps, rows, wx, wy = adjoint.shape
    zc_rows, ncol = coarse_velocity.shape
    half_y = wy // 2
    tiles = ncol // wy
    pairs_x = shots * tiles
    chans = filters.shape[0]
    count = receiver_cells.shape[1]
    out_x, deep = 2 * tiles + 2, 2 * zc_rows
    vmem = pl.BlockSpec(memory_space=pltpu.VMEM)
    smem = pl.BlockSpec(memory_space=pltpu.SMEM)
    hbm = pl.BlockSpec(memory_space=pltpu.HBM)
    trace_rows = -(-steps // 8) * 8
    dma = pltpu.SemaphoreType.DMA
    field = pltpu.VMEM((rows + 2 * HALO, wx, wy), f32)
    scratch = (
        [field] * (steps + 2)
        + [pltpu.VMEM((rows, wx, wy), f32)] * steps
        + [
            pltpu.VMEM((zc_rows, ncol), f32),
            pltpu.VMEM(filters.shape, f32),
            pltpu.SMEM(wavelet.shape, f32),
            pltpu.SMEM(receiver_cells.shape, i32),
            pltpu.VMEM(receiver_cells.shape, i32),
            pltpu.VMEM((zc_rows, wx, wy), f32),
            pltpu.VMEM((zc_rows, wx, wy), f32),
            pltpu.VMEM((wx, 3 * wx), bf16),
            pltpu.VMEM((3 * wy, wy), bf16),
            pltpu.VMEM((4, wx, wy), f32),
            pltpu.VMEM((shots, zc_rows, ncol), f32),
            pltpu.VMEM((2, pairs_x * zc_rows, wy), f32),
            pltpu.VMEM((tiles + 2, zc_rows, wy), f32),
            pltpu.VMEM((tiles + 2, zc_rows, wy), f32),
            pltpu.VMEM((2 * tiles + 4, 3 * zc_rows, wy), f32),
            pltpu.VMEM((out_x * deep, 9 * wy), bf16),
            pltpu.VMEM((9 * wy, chans * half_y), bf16),
            pltpu.VMEM((9 * wy, chans * half_y), bf16),
            pltpu.VMEM((out_x * deep, 9 * wy), f32),
            pltpu.VMEM((wx, wy), f32),
            pltpu.VMEM((pairs_x * zc_rows, wy), f32),
            pltpu.VMEM((shots, tiles * zc_rows, wy), f32),
            pltpu.VMEM((steps, count, wy), f32),
            pltpu.VMEM((trace_rows, count), f32),
            pltpu.VMEM((trace_rows, count), f32),
            dma((7 + steps,)),
            dma((2,)),
            dma((steps,)),
            dma((steps,)),
            dma((shots,)),
            dma((shots,)),
            dma((shots,)),
            dma((shots,)),
            dma((2,)),
            dma((2,)),
        ]
    )
    out_shape = (
        jax.ShapeDtypeStruct((zc_rows, ncol), f32),
        jax.ShapeDtypeStruct(wave_prev.shape, f32),
        jax.ShapeDtypeStruct(wave_now.shape, f32),
        jax.ShapeDtypeStruct((1, steps, count), f32),
    )
    results = pl.pallas_call(
        functools.partial(kernel, shots, steps),
        out_shape=out_shape,
        in_specs=[hbm, hbm, hbm, hbm, hbm, hbm, smem, hbm],
        out_specs=(vmem, hbm, hbm, vmem),
        scratch_shapes=scratch,
        compiler_params=pltpu.CompilerParams(
            collective_id=0, has_side_effects=True, vmem_limit_bytes=GRANT
        ),
    )(
        wave_prev, wave_now, adjoint, coarse_velocity, filters, wavelet, source_cell,
        receiver_cells,
    )
    return pl.pallas_call(
        store_kernel,
        out_shape=out_shape,
        in_specs=[hbm] * 4,
        out_specs=(hbm,) * 4,
        scratch_shapes=[pltpu.VMEM(x.shape, f32) for x in out_shape] + [dma((4, 4)), dma((4, 4))],
        compiler_params=pltpu.CompilerParams(vmem_limit_bytes=GRANT),
    )(*results)


def solution(mesh):
    return jax.shard_map(
        functools.partial(body, mesh.shape["shot"]),
        mesh=mesh,
        in_specs=(
            P(("grp", "shot"), "depth", None, None),
            P(("grp", "shot"), "depth", None, None),
            P(("grp", "shot"), None, "depth", None, None),
            P(("grp", "depth"), "shot"),
            P(),
            P(("grp", "shot"), None),
            P(("grp", "shot")),
            P(("grp", "shot"), None),
        ),
        out_specs=(
            P(("grp", "depth"), "shot"),
            P(("grp", "shot"), "depth", None, None),
            P(("grp", "shot"), "depth", None, None),
            P(("grp", "shot"), None, None),
        ),
        check_vma=False,
    )
```
